256 devices in a mesh: pb: 16 (over x, y), aux: 16 (over z, core).
Axes of the slice: x: 4, y: 4, z: 8, core: 2. Of those that a mesh axis runs over, the one named last changes fastest.
Arguments:
- ao_blocks: float32 [16, 4, 640, 2, 6400], P('pb', None, 'aux'), may hold values from -1 to 1
- occ_coef: float32 [27, 2, 80, 16], replicated, may hold values from -0.625 to 0.625
- vir_coef: float32 [27, 2, 80, 64], replicated, may hold values from -0.625 to 0.625
- occ_energy: float32 [27, 16], replicated, may hold values from -2.5 to -0.5
- vir_energy: float32 [27, 64], replicated, may hold values from 0.5 to 4
- kpoint_diff: int32 [27, 27], replicated, may hold values from 0 to 26, as said below
- transfer_label: int32 [16], replicated, may hold values from 1 to 26, as said below
- chosen_rows: int32 [16, 4], replicated, may hold values from 0 to 26, as said below
Outputs:
- amplitudes: float32 [16, 2, 2, 2, 16, 16, 4096], P('pb', None, None, None, 'aux')
The draws below stay inside these ranges and needn't reach their ends.
Inputs may be any that keep to these rules, and one draw needn't show every extreme that they name: The k-points are the points of a 3 x 3 x 3 periodic mesh under a relabeling drawn from the seed, with label 0 for the zero transfer; kpoint_diff[k, q] is the label of k - q modulo the mesh, so it is a group table. `transfer_label`: the labels are nonzero transfers, all different; slots 2m and 2m + 1 hold opposite transfers, q and -q. `chosen_rows`: the four entries of each row are different k labels.
All inputs are finite; a program needn't handle non-finite values.
Results may differ from the reference program's by a relative error of at most 0.0001.
Values sent between devices are 32-bit elements; how exact they have to be, the bound alone decides.
A program may use at most 128 MiB of HBM per device.

```python
import jax
import jax.numpy as jnp
import numpy as np
from jax import lax

NK = 27
NOCC = 16
NVIR = 64
NAO = 80
NAUX = 640
Q = 16


def mesh_labels(key):
    rest = jax.random.permutation(jax.random.fold_in(key, 7), NK - 1).astype(jnp.int32) + 1
    return jnp.concatenate([jnp.zeros((1,), jnp.int32), rest]).astype(jnp.int32)


def negate_flat(flat_index):
    xpos = flat_index // 9
    ypos = flat_index // 3 % 3
    zpos = flat_index % 3
    return (3 - xpos) % 3 * 9 + (3 - ypos) % 3 * 3 + (3 - zpos) % 3


def draw_kpoint_diff(key, part):
    labels = mesh_labels(key)
    inverse = jnp.argsort(labels).astype(jnp.int32)
    first = inverse[:, None]
    second = inverse[None, :]
    xdiff = (first // 9 - second // 9) % 3
    ydiff = (first // 3 % 3 - second // 3 % 3) % 3
    zdiff = (first % 3 - second % 3) % 3
    return labels[xdiff * 9 + ydiff * 3 + zdiff].astype(jnp.int32)


def draw_transfer_label(key, part):
    labels = mesh_labels(key)
    inverse = jnp.argsort(labels).astype(jnp.int32)
    negs = np.array([(3 - f // 9) % 3 * 9 + (3 - f // 3 % 3) % 3 * 3 + (3 - f % 3) % 3 for f in range(27)])
    chosen = np.array([f for f in range(1, 27) if f < negs[f]], dtype=np.int32)
    chosen_arr = jnp.asarray(chosen)
    top_flat = inverse[NK - 1]
    top_rep = jnp.minimum(top_flat, negate_flat(top_flat))
    top_pos = jnp.sum((chosen_arr < top_rep).astype(jnp.int32)).astype(jnp.int32)
    order = jax.random.permutation(jax.random.fold_in(key, 11), 13).astype(jnp.int32)
    where_top = jnp.argmax((order == top_pos).astype(jnp.int32)).astype(jnp.int32)
    order = order.at[where_top].set(order[0]).at[0].set(top_pos)
    picked = chosen_arr[order[:Q // 2]]
    opposite = negate_flat(picked)
    pairs = jnp.stack([labels[picked], labels[opposite]], axis=1)
    return pairs.reshape(Q).astype(jnp.int32)


def draw_chosen_rows(key, part):
    keys = jax.random.split(jax.random.fold_in(key, 13), Q)
    return jax.vmap(lambda single: jax.random.permutation(single, NK)[:4])(keys).astype(jnp.int32)


def block_levels(own_key, extent, shards, low, high):
    gain = 1.0
    for dim, blocks in shards:
        heights = jax.random.uniform(jax.random.fold_in(jax.random.fold_in(own_key, 6), dim), (blocks,), jnp.float32, low / len(shards), high / len(shards))
        gain = gain * jnp.repeat(jnp.exp(heights), extent[dim] // blocks).reshape((-1,) + (1,) * (len(extent) - 1 - dim))
    return gain


def gaussian(rng, dims, scale, most, pieces=(), held_as=jnp.bfloat16):
    gain = block_levels(rng, dims, pieces, -0.22, 0.18) if pieces else 1.0
    values = jax.random.normal(rng, dims, jnp.float32) * scale * gain
    return jnp.minimum(jnp.maximum(values, -most), most).astype(held_as)


def setup_inputs(seed: int = 0) -> dict:
    seeds = jax.random.split(jax.random.key(seed), 9)
    return {
        "ao_blocks": gaussian(seeds[0], (Q, 4, NAUX, 2, NAO * NAO), (NAUX // 16) ** -0.5, 1.0, ((0, 16), (2, 16)), jnp.float32),
        "occ_coef": gaussian(seeds[1], (NK, 2, NAO, NOCC), NAO ** -0.5, 0.625, (), jnp.float32),
        "vir_coef": gaussian(seeds[2], (NK, 2, NAO, NVIR), NAO ** -0.5, 0.625, (), jnp.float32),
        "occ_energy": jnp.clip(jax.random.uniform(seeds[3], (NK, NOCC), jnp.float32, -2.5, -0.5), -2.5, -0.5),
        "vir_energy": jnp.clip(jax.random.uniform(seeds[4], (NK, NVIR), jnp.float32, 0.5, 4.0), 0.5, 4.0),
        "kpoint_diff": draw_kpoint_diff(jax.random.fold_in(seeds[8], 71), 0),
        "transfer_label": draw_transfer_label(jax.random.fold_in(seeds[8], 71), 0),
        "chosen_rows": draw_chosen_rows(jax.random.fold_in(seeds[8], 71), 0),
    }


def to_orbitals(blocks, occ_sel, vir_sel):
    highest = lax.Precision.HIGHEST
    ao_width = occ_sel.shape[2]
    complex_ao = blocks.reshape(blocks.shape[0], blocks.shape[1], 2, ao_width, ao_width)
    real_ao = complex_ao[:, :, 0]
    imag_ao = complex_ao[:, :, 1]
    occ_real = occ_sel[:, 0]
    occ_imag = occ_sel[:, 1]
    half_real = jnp.einsum('smi,spmn->spin', occ_real, real_ao, precision=highest) + jnp.einsum('smi,spmn->spin', occ_imag, imag_ao, precision=highest)
    half_imag = jnp.einsum('smi,spmn->spin', occ_real, imag_ao, precision=highest) - jnp.einsum('smi,spmn->spin', occ_imag, real_ao, precision=highest)
    vir_real = vir_sel[:, 0]
    vir_imag = vir_sel[:, 1]
    full_real = jnp.einsum('spin,sna->spia', half_real, vir_real, precision=highest) - jnp.einsum('spin,sna->spia', half_imag, vir_imag, precision=highest)
    full_imag = jnp.einsum('spin,sna->spia', half_real, vir_imag, precision=highest) + jnp.einsum('spin,sna->spia', half_imag, vir_real, precision=highest)
    return jnp.concatenate([full_real, full_imag], axis=3)


def pair_sums(left_side, right_side, vir_width):
    highest = lax.Precision.HIGHEST
    pattern = 'spia,tpjb->stijab'
    left_real = left_side[..., :vir_width]
    left_imag = left_side[..., vir_width:]
    right_real = right_side[..., :vir_width]
    right_imag = right_side[..., vir_width:]
    real_part = jnp.einsum(pattern, left_real, right_real, precision=highest) - jnp.einsum(pattern, left_imag, right_imag, precision=highest)
    imag_part = jnp.einsum(pattern, left_real, right_imag, precision=highest) + jnp.einsum(pattern, left_imag, right_real, precision=highest)
    return real_part, imag_part


def make_amplitudes(real_part, imag_part, occ_left, occ_right, vir_left, vir_right):
    denominator = (occ_left[:, None, :, None, None, None] + occ_right[None, :, None, :, None, None]
                   - vir_left[:, None, None, None, :, None] - vir_right[None, :, None, None, None, :])
    result = jnp.stack([real_part / denominator, imag_part / denominator])
    shape_now = result.shape
    return result.reshape(shape_now[0], shape_now[1], shape_now[2], shape_now[3], shape_now[4], shape_now[5] * shape_now[6])


def reference(ao_blocks, occ_coef, vir_coef, occ_energy, vir_energy, kpoint_diff, transfer_label, chosen_rows):
    vir_width = vir_coef.shape[3]
    orbitals = []
    for position in range(Q):
        own_rows = chosen_rows[position]
        own_vir = kpoint_diff[own_rows, transfer_label[position]]
        orbitals.append(to_orbitals(ao_blocks[position], occ_coef[own_rows], vir_coef[own_vir]))
    outputs = []
    for position in range(Q):
        partner = position ^ 1
        own_rows = chosen_rows[position]
        own_vir = kpoint_diff[own_rows, transfer_label[position]]
        other_rows = chosen_rows[partner]
        other_vir = kpoint_diff[other_rows, transfer_label[partner]]
        real_part, imag_part = pair_sums(orbitals[position][0:2], orbitals[partner][2:4], vir_width)
        outputs.append(make_amplitudes(real_part, imag_part, occ_energy[own_rows[0:2]], occ_energy[other_rows[2:4]],
                                       vir_energy[own_vir[0:2]], vir_energy[other_vir[2:4]]))
    return jnp.stack(outputs)
```

```python
import functools

import jax
import jax.numpy as jnp
from jax import lax
from jax.experimental import pallas as pl
from jax.experimental.pallas import tpu as pltpu
from jax.sharding import PartitionSpec as P

MESH = pl.DeviceIdType.MESH
F32 = jnp.float32
BF16 = jnp.bfloat16

TILES = tuple(
    tuple((m, 80 * m - 128 * k) for m in range(8) if -80 < 80 * m - 128 * k < 128)
    for k in range(5)
)


def halves(x):
    hi = x.astype(BF16)
    return hi, (x - hi.astype(F32)).astype(BF16)


def dot(x, y):
    return jnp.dot(x, y, preferred_element_type=F32)


def swap_sides(x):
    return pltpu.roll(x, 64, 1)


def fill_weights(vir_ref, w_hi, w_lo):
    vre, vim = vir_ref[0, 0], vir_ref[0, 1]
    pad = jnp.zeros((128, 48), F32)
    for part, top, bottom in ((0, vre, vim), (1, -vim, vre)):
        stacked = jnp.concatenate([jnp.concatenate([top, bottom], 0), pad], 1)
        hi, lo = halves(stacked.T[:80])
        for k, blocks in enumerate(TILES):
            for b, (_, start) in enumerate(blocks):
                first, last = max(start, 0), min(start + 80, 128)
                to = (k, slice(part * 128 + first, part * 128 + last), slice(128 * b, 128 * b + 128))
                w_hi[to] = hi[first - start : last - start]
                w_lo[to] = lo[first - start : last - start]


def orbitals(s, ao_ref, occ_ref, vir_ref, put, w_hi, w_lo, x_hi, x_lo, t1):
    fill_weights(vir_ref, w_hi, w_lo)

    def load(pair, _):
        for k in range(5):
            sides = []
            for part in range(2):
                sides.append(
                    jnp.concatenate(
                        [
                            ao_ref[0, pl.ds(((pair * 2 + h) * 5 + k) * 2 + part, 40, stride=100), :]
                            for h in range(2)
                        ],
                        0,
                    )
                )
            hi, lo = halves(jnp.concatenate(sides, 1))
            at = pl.ds(pl.multiple_of(pair * 80, 16), 80)
            x_hi[k, at, :] = hi
            x_lo[k, at, :] = lo
        return 0

    lax.fori_loop(0, 5, load, 0)
    carry = None
    for k, blocks in enumerate(TILES):
        width = 128 * len(blocks)
        wh, wl = w_hi[k, :, :width], w_lo[k, :, :width]
        xh, xl = x_hi[k], x_lo[k]
        y = dot(xh, wh) + dot(xh, wl) + dot(xl, wh)
        for b, (m, start) in enumerate(blocks):
            value = y[:, 128 * b : 128 * b + 128]
            if start < 0:
                value = value + carry
            if start + 80 > 128:
                carry = value
                continue
            for g in range(10):
                t1[pl.ds(8 * g + m, 40, stride=80), :] = value[40 * g : 40 * g + 40]

    occ = jnp.concatenate([occ_ref[0, 0], occ_ref[0, 1]], 0)
    c_hi, c_lo = halves(occ)
    c_both = jnp.concatenate([c_hi, c_lo], 0)
    sign = jnp.where(lax.broadcasted_iota(jnp.int32, (16, 128), 1) < 64, 1.0, -1.0).astype(F32)

    def second(pair, _):
        rows = t1[pl.ds(pl.multiple_of(pair * 160, 8), 160), :]
        hi, lo = halves(jnp.concatenate([rows[:80], rows[80:]], 1))
        both = dot(c_both, hi)
        u = both[:32] + both[32:] + dot(c_hi, lo)
        for h in range(2):
            ure, uim = u[:16, 128 * h : 128 * h + 128], u[16:, 128 * h : 128 * h + 128]
            put(pair * 2 + h, ure + sign * swap_sides(uim))
        return 0

    lax.fori_loop(0, 20, second, 0, unroll=4)


def step_one_kernel(
    place, rows, diff, label, ao_ref, occ_ref, vir_ref, occ_e, vir_e, lr_ref, base_ref, occr_ref,
    w_hi, w_lo, x_hi, x_lo, t1,
):
    s = pl.program_id(0)

    @pl.when(s == 0)
    def _():
        w_hi[...] = jnp.zeros_like(w_hi)
        w_lo[...] = jnp.zeros_like(w_lo)
        slot, i = place[0], place[1]
        other = slot + 1 - 2 * (slot % 2)
        col = lax.broadcasted_iota(jnp.int32, (32, 64), 1)
        row = lax.broadcasted_iota(jnp.int32, (32, 64), 0)
        low = lax.broadcasted_iota(jnp.int32, (32, 128), 1) < 64
        lane = lax.broadcasted_iota(jnp.int32, (1, 16), 1)
        eye = lax.broadcasted_iota(jnp.int32, (16, 16), 0) == lax.broadcasted_iota(jnp.int32, (16, 16), 1)
        for b in range(2):
            ki = rows[slot, b]
            ka = diff[ki, label[slot]]
            occ_left = jnp.sum(jnp.where(lane == i, occ_e[pl.ds(ki, 1), :], 0.0), axis=1, keepdims=True)
            line = vir_e[pl.ds(ka, 1), :]
            even = jnp.sum(jnp.where(col == 2 * row, line, 0.0), axis=1, keepdims=True)
            odd = jnp.sum(jnp.where(col == 2 * row + 1, line, 0.0), axis=1, keepdims=True)
            left = occ_left - jnp.where(low, even, odd)
            for t in range(2):
                kj = rows[other, 2 + t]
                kb = diff[kj, label[other]]
                right = vir_e[pl.ds(kb, 1), :]
                base_ref[2 * b + t] = left - jnp.concatenate([right, right], 1)
                if b == 0:
                    occ_right = jnp.sum(jnp.where(eye, occ_e[pl.ds(kj, 1), :], 0.0), axis=1, keepdims=True)
                    occr_ref[t] = jnp.broadcast_to(occ_right, (16, 128))

    def put(p, value):
        lr_ref[pl.ds(s * 640 + p, 16, stride=40), :] = value

    orbitals(s, ao_ref, occ_ref, vir_ref, put, w_hi, w_lo, x_hi, x_lo, t1)


def step_one(place, rows, diff, label, ao, occ, vir, occ_e, vir_e):
    def k_of(s, place, rows, diff, label):
        return rows[place[0], s]

    def occ_at(s, *scalars):
        return (k_of(s, *scalars), 0, 0, 0)

    def vir_at(s, place, rows, diff, label):
        return (diff[rows[place[0], s], label[place[0]]], 0, 0, 0)

    def whole(*shape):
        return pl.BlockSpec(shape, lambda s, *_: (0,) * len(shape))

    return pl.pallas_call(
        step_one_kernel,
        out_shape=(
            jax.ShapeDtypeStruct((2560, 128), F32),
            jax.ShapeDtypeStruct((4, 32, 128), F32),
            jax.ShapeDtypeStruct((2, 16, 128), F32),
        ),
        grid_spec=pltpu.PrefetchScalarGridSpec(
            num_scalar_prefetch=4,
            grid=(4,),
            in_specs=[
                pl.BlockSpec((1, 4000, 128), lambda s, *_: (s, 0, 0)),
                pl.BlockSpec((1, 2, 16, 80), occ_at),
                pl.BlockSpec((1, 2, 64, 80), vir_at),
                whole(27, 16),
                whole(27, 64),
            ],
            out_specs=(whole(2560, 128), whole(4, 32, 128), whole(2, 16, 128)),
            scratch_shapes=[
                pltpu.VMEM((5, 256, 384), BF16),
                pltpu.VMEM((5, 256, 384), BF16),
                pltpu.VMEM((5, 400, 256), BF16),
                pltpu.VMEM((5, 400, 256), BF16),
                pltpu.VMEM((3200, 128), F32),
            ],
        ),
        compiler_params=pltpu.CompilerParams(vmem_limit_bytes=40 * 2**20),
        cost_estimate=pl.CostEstimate(flops=2 * 10**9, bytes_accessed=9 * 10**6, transcendentals=0),
        name="step_one",
    )(place, rows, diff, label, ao, occ, vir, occ_e, vir_e)


POS = {0: 0, 1: 1, -1: 2, 2: 3, -2: 4, 3: 5, -3: 6, 4: 7, -4: 7}
STAGES = ((0, 240), (240, 400), (400, 640))


def pair_kernel(
    lr_ref, base_ref, occr_ref, out_ref, rbuf, lbuf, lt_hi, lt_lo, ybuf,
    par_send, par_recv, hop_send, hop_recv, sib_send, sib_recv, l_send, l_recv, own_sem,
):
    pb, aux = lax.axis_index("pb"), lax.axis_index("aux")
    z, c = aux // 2, aux % 2
    partner = pb + 1 - 2 * (pb % 2)
    sibling = aux + 1 - 2 * c

    def at_z(dz, core):
        return lax.rem(z + dz + 8, 8) * 2 + core

    barrier = pltpu.get_barrier_semaphore()
    for far in range(1, 16):
        pl.semaphore_signal(barrier, inc=1, device_id={"aux": lax.rem(aux + far, 16)}, device_id_type=MESH)
    pl.semaphore_signal(barrier, inc=1, device_id={"pb": partner}, device_id_type=MESH)
    pl.semaphore_wait(barrier, 16)

    def place(pos, core):
        return pl.ds(pl.multiple_of(pos * 80 + core * 40, 8), 40)

    def chunk(pos, t):
        return rbuf.at[pl.ds(16 * t, 16), place(pos, c), :]

    def partner_copy(t):
        return pltpu.make_async_remote_copy(
            lr_ref.at[2 + t], chunk(0, t), par_send.at[t], par_recv.at[t],
            device_id={"pb": partner}, device_id_type=MESH,
        )

    def hop_copy(way, d, t):
        step = 1 - 2 * way
        return pltpu.make_async_remote_copy(
            chunk(POS[-step * (d - 1)], t), chunk(POS[-step * d], t),
            hop_send.at[way, d - 1, t], hop_recv.at[way, d - 1, t],
            device_id={"aux": at_z(step, c)}, device_id_type=MESH,
        )

    def sibling_copy(pos, t):
        return pltpu.make_async_remote_copy(
            chunk(pos, t), chunk(pos, t), sib_send.at[pos, t], sib_recv.at[pos, t],
            device_id={"aux": sibling}, device_id_type=MESH,
        )

    def row_copy(dz, cross):
        core = c + cross * (1 - 2 * c)
        to = at_z(dz, core)
        pos = POS[-dz]
        src, dst = lr_ref.at[pl.ds(0, 2), to], lbuf.at[:, place(pos, c), :]
        if dz == 0 and cross == 0:
            return pltpu.make_async_copy(src, dst, own_sem)
        return pltpu.make_async_remote_copy(
            src, dst, l_send.at[pos, cross], l_recv.at[pos, cross],
            device_id={"aux": to}, device_id_type=MESH,
        )

    def has_hop(way, d, t):
        return d < 4 or t == way

    partners = [partner_copy(t) for t in range(2)]
    for copy in partners:
        copy.start()
    rows = {(dz, cross): row_copy(dz, cross) for dz in (4, 3, -3, 2, -2, 1, -1, 0) for cross in range(2)}
    for copy in rows.values():
        copy.start()

    sent = []

    def send(copy):
        copy.start()
        sent.append(copy)

    for t in range(2):
        partners[t].wait_recv()
        for way in range(2):
            send(hop_copy(way, 1, t))
        send(sibling_copy(0, t))

    def relay(d):
        for t in range(2):
            for way in range(2):
                if not has_hop(way, d, t):
                    continue
                hop_copy(way, d, t).wait_recv()
                if d < 4 and has_hop(way, d + 1, t):
                    send(hop_copy(way, d + 1, t))
                send(sibling_copy(POS[-d if way == 0 else d], t))

    def left_sides():
        for (dz, cross), copy in rows.items():
            if dz == 0 and cross == 0:
                copy.wait()
            else:
                copy.wait_recv()
        for n, (first, last) in enumerate(STAGES):
            for s in range(2):
                part = lbuf[s, first:last, :]
                part = jnp.concatenate([part, jnp.zeros((256 - (last - first), 128), F32)], 0)
                hi, lo = halves(part.T)
                lt_hi[n, 128 * s : 128 * s + 128, :] = hi
                lt_lo[n, 128 * s : 128 * s + 128, :] = lo

    low = lax.broadcasted_iota(jnp.int32, (32, 128), 1) < 64

    def finish(n):
        t, j = n // 16, n % 16
        for s in range(2):
            def half(part, odd):
                return ybuf[n, pl.ds(128 * s + 64 * part + odd, 32, stride=2), :]

            re_e, re_d, im_e, im_d = half(0, 0), half(0, 1), half(1, 0), half(1, 1)
            inverse = 1.0 / (base_ref[2 * s + t] + occr_ref[t, pl.ds(j, 1), :])
            real = jnp.where(low, re_e, swap_sides(re_d)) - jnp.where(low, swap_sides(im_e), im_d)
            imag = jnp.where(low, swap_sides(re_e), re_d) + jnp.where(low, im_e, swap_sides(im_d))
            for part, value in enumerate((real, imag)):
                first = ((part * 2 + s) * 2 + t) * 512 + (j // 8) * 256 + j % 8
                out_ref[pl.ds(first, 32, stride=8), :] = value * inverse

    def multiply(stage):
        first, last = STAGES[stage]
        width = last - first

        def body(pair, _):
            r = jnp.concatenate([rbuf[pair * 2 + h, first:last, :] for h in range(2)], 1)
            hi, lo = halves(r)
            lh, ll = lt_hi[stage, :, :width], lt_lo[stage, :, :width]
            y = dot(lh, hi) + dot(ll, hi) + dot(lh, lo)
            for h in range(2):
                value = y[:, 128 * h : 128 * h + 128]
                if stage > 0:
                    value = value + ybuf[pair * 2 + h]
                ybuf[pair * 2 + h] = value
                if stage == 2:
                    finish(pair * 2 + h)
            return 0

        lax.fori_loop(0, 16, body, 0)

    def from_sibling(*positions):
        for pos in positions:
            for t in range(2):
                sibling_copy(pos, t).wait_recv()

    relay(1)
    left_sides()
    from_sibling(0, 1, 2)
    relay(2)
    multiply(0)
    relay(3)
    from_sibling(3, 4)
    multiply(1)
    relay(4)
    from_sibling(5, 6, 7)
    multiply(2)
    for copy in partners + sent:
        copy.wait_send()
    for (dz, cross), copy in rows.items():
        if dz != 0 or cross != 0:
            copy.wait_send()


def pair_sums(lr, base, occr):
    vmem = pl.BlockSpec(memory_space=pltpu.VMEM)
    dma = pltpu.SemaphoreType.DMA
    return pl.pallas_call(
        pair_kernel,
        out_shape=jax.ShapeDtypeStruct((4096, 128), F32),
        in_specs=[pl.BlockSpec(memory_space=pl.ANY), vmem, vmem],
        out_specs=vmem,
        scratch_shapes=[
            pltpu.VMEM((32, 640, 128), F32),
            pltpu.VMEM((2, 640, 128), F32),
            pltpu.VMEM((3, 256, 256), BF16),
            pltpu.VMEM((3, 256, 256), BF16),
            pltpu.VMEM((32, 256, 128), F32),
            dma((2,)), dma((2,)),
            dma((2, 4, 2)), dma((2, 4, 2)),
            dma((8, 2)), dma((8, 2)),
            dma((8, 2)), dma((8, 2)),
            dma,
        ],
        compiler_params=pltpu.CompilerParams(
            collective_id=0, has_side_effects=True, vmem_limit_bytes=48 * 2**20
        ),
        cost_estimate=pl.CostEstimate(flops=4 * 10**9, bytes_accessed=4 * 10**6, transcendentals=0),
        name="pair_sums",
    )(lr, base, occr)


def per_device(
    ao_blocks, occ_coef, vir_coef, occ_energy, vir_energy, kpoint_diff, transfer_label, chosen_rows
):
    place = jnp.stack([lax.axis_index("pb"), lax.axis_index("aux")]).astype(jnp.int32)
    ao = ao_blocks.reshape(4, 40, 2, 50, 128).transpose(0, 1, 3, 2, 4).reshape(4, 4000, 128)
    lr, base, occr = step_one(
        place, chosen_rows, kpoint_diff, transfer_label, ao,
        occ_coef.swapaxes(2, 3), vir_coef.swapaxes(2, 3), occ_energy, vir_energy,
    )
    out = pair_sums(lr.reshape(4, 16, 40, 128), base, occr)
    out = out.reshape(2, 2, 2, 2, 32, 8, 128).transpose(0, 1, 2, 3, 5, 4, 6)
    return out.reshape(1, 2, 2, 2, 1, 16, 4096)


def solution(mesh):
    in_specs = (P("pb", None, "aux", None, None), P(), P(), P(), P(), P(), P(), P())
    out_specs = P("pb", None, None, None, "aux", None, None)
    return jax.shard_map(
        per_device, mesh=mesh, in_specs=in_specs, out_specs=out_specs, check_vma=False
    )
```

```python
import functools

import jax
import jax.numpy as jnp
from jax import lax
from jax.experimental import pallas as pl
from jax.experimental.layout import Layout, with_layout_constraint
from jax.experimental.pallas import tpu as pltpu
from jax.sharding import PartitionSpec as P

MESH = pl.DeviceIdType.MESH
F32 = jnp.float32
BF16 = jnp.bfloat16

TILES = tuple(
    tuple((m, 80 * m - 128 * k) for m in range(8) if -80 < 80 * m - 128 * k < 128)
    for k in range(5)
)


def halves(x):
    hi = x.astype(BF16)
    return hi, (x - hi.astype(F32)).astype(BF16)


def dot(x, y):
    return jnp.dot(x, y, preferred_element_type=F32)


def swap_sides(x):
    return pltpu.roll(x, 64, 1)


def fill_weights(vir_ref, w_hi, w_lo):
    vre, vim = vir_ref[0, 0], vir_ref[0, 1]
    pad = jnp.zeros((128, 48), F32)
    for part, top, bottom in ((0, vre, vim), (1, -vim, vre)):
        stacked = jnp.concatenate([jnp.concatenate([top, bottom], 0), pad], 1)
        hi, lo = halves(stacked.T[:80])
        for k, blocks in enumerate(TILES):
            for b, (_, start) in enumerate(blocks):
                first, last = max(start, 0), min(start + 80, 128)
                to = (k, slice(part * 128 + first, part * 128 + last), slice(128 * b, 128 * b + 128))
                w_hi[to] = hi[first - start : last - start]
                w_lo[to] = lo[first - start : last - start]


def orbitals(s, ao_ref, occ_ref, vir_ref, put, w_hi, w_lo, x_hi, x_lo, t1):
    fill_weights(vir_ref, w_hi, w_lo)

    def load(pair, _):
        for k in range(5):
            sides = []
            for part in range(2):
                sides.append(
                    jnp.concatenate(
                        [
                            ao_ref[0, pl.ds(((pair * 2 + h) * 5 + k) * 2 + part, 40, stride=100), :]
                            for h in range(2)
                        ],
                        0,
                    )
                )
            hi, lo = halves(jnp.concatenate(sides, 1))
            at = pl.ds(pl.multiple_of(pair * 80, 16), 80)
            x_hi[k, at, :] = hi
            x_lo[k, at, :] = lo
        return 0

    lax.fori_loop(0, 5, load, 0)
    carry = None
    for k, blocks in enumerate(TILES):
        width = 128 * len(blocks)
        wh, wl = w_hi[k, :, :width], w_lo[k, :, :width]
        xh, xl = x_hi[k], x_lo[k]
        y = dot(xh, wh) + dot(xh, wl) + dot(xl, wh)
        for b, (m, start) in enumerate(blocks):
            value = y[:, 128 * b : 128 * b + 128]
            if start < 0:
                value = value + carry
            if start + 80 > 128:
                carry = value
                continue
            for g in range(10):
                t1[pl.ds(8 * g + m, 40, stride=80), :] = value[40 * g : 40 * g + 40]

    occ = jnp.concatenate([occ_ref[0, 0], occ_ref[0, 1]], 0)
    c_hi, c_lo = halves(occ)
    c_both = jnp.concatenate([c_hi, c_lo], 0)
    sign = jnp.where(lax.broadcasted_iota(jnp.int32, (16, 128), 1) < 64, 1.0, -1.0).astype(F32)

    def second(pair, _):
        rows = t1[pl.ds(pl.multiple_of(pair * 160, 8), 160), :]
        hi, lo = halves(jnp.concatenate([rows[:80], rows[80:]], 1))
        both = dot(c_both, hi)
        u = both[:32] + both[32:] + dot(c_hi, lo)
        for h in range(2):
            ure, uim = u[:16, 128 * h : 128 * h + 128], u[16:, 128 * h : 128 * h + 128]
            put(pair * 2 + h, ure + sign * swap_sides(uim))
        return 0

    lax.fori_loop(0, 20, second, 0, unroll=4)


def step_one_kernel(
    place, rows, diff, label, ao_ref, occ_ref, vir_ref, occ_e, vir_e, lr_ref, base_ref, occr_ref,
    w_hi, w_lo, x_hi, x_lo, t1,
):
    s = pl.program_id(0)

    @pl.when(s == 0)
    def _():
        w_hi[...] = jnp.zeros_like(w_hi)
        w_lo[...] = jnp.zeros_like(w_lo)
        slot, i = place[0], place[1]
        other = slot + 1 - 2 * (slot % 2)
        col = lax.broadcasted_iota(jnp.int32, (32, 64), 1)
        row = lax.broadcasted_iota(jnp.int32, (32, 64), 0)
        low = lax.broadcasted_iota(jnp.int32, (32, 128), 1) < 64
        lane = lax.broadcasted_iota(jnp.int32, (1, 16), 1)
        eye = lax.broadcasted_iota(jnp.int32, (16, 16), 0) == lax.broadcasted_iota(jnp.int32, (16, 16), 1)
        for b in range(2):
            ki = rows[slot, b]
            ka = diff[ki, label[slot]]
            occ_left = jnp.sum(jnp.where(lane == i, occ_e[pl.ds(ki, 1), :], 0.0), axis=1, keepdims=True)
            line = vir_e[pl.ds(ka, 1), :]
            even = jnp.sum(jnp.where(col == 2 * row, line, 0.0), axis=1, keepdims=True)
            odd = jnp.sum(jnp.where(col == 2 * row + 1, line, 0.0), axis=1, keepdims=True)
            left = occ_left - jnp.where(low, even, odd)
            for t in range(2):
                kj = rows[other, 2 + t]
                kb = diff[kj, label[other]]
                right = vir_e[pl.ds(kb, 1), :]
                base_ref[2 * b + t] = left - jnp.concatenate([right, right], 1)
                if b == 0:
                    occ_right = jnp.sum(jnp.where(eye, occ_e[pl.ds(kj, 1), :], 0.0), axis=1, keepdims=True)
                    occr_ref[t] = jnp.broadcast_to(occ_right, (16, 128))

    def put(p, value):
        lr_ref[pl.ds(s * 640 + p, 16, stride=40), :] = value

    orbitals(s, ao_ref, occ_ref, vir_ref, put, w_hi, w_lo, x_hi, x_lo, t1)


def step_one(place, rows, diff, label, ao, occ, vir, occ_e, vir_e):
    def k_of(s, place, rows, diff, label):
        return rows[place[0], s]

    def occ_at(s, *scalars):
        return (k_of(s, *scalars), 0, 0, 0)

    def vir_at(s, place, rows, diff, label):
        return (diff[rows[place[0], s], label[place[0]]], 0, 0, 0)

    def whole(*shape):
        return pl.BlockSpec(shape, lambda s, *_: (0,) * len(shape))

    return pl.pallas_call(
        step_one_kernel,
        out_shape=(
            jax.ShapeDtypeStruct((2560, 128), F32),
            jax.ShapeDtypeStruct((4, 32, 128), F32),
            jax.ShapeDtypeStruct((2, 16, 128), F32),
        ),
        grid_spec=pltpu.PrefetchScalarGridSpec(
            num_scalar_prefetch=4,
            grid=(4,),
            in_specs=[
                pl.BlockSpec((1, 4000, 128), lambda s, *_: (s, 0, 0)),
                pl.BlockSpec((1, 2, 16, 80), occ_at),
                pl.BlockSpec((1, 2, 64, 80), vir_at),
                whole(27, 16),
                whole(27, 64),
            ],
            out_specs=(whole(2560, 128), whole(4, 32, 128), whole(2, 16, 128)),
            scratch_shapes=[
                pltpu.VMEM((5, 256, 384), BF16),
                pltpu.VMEM((5, 256, 384), BF16),
                pltpu.VMEM((5, 400, 256), BF16),
                pltpu.VMEM((5, 400, 256), BF16),
                pltpu.VMEM((3200, 128), F32),
            ],
        ),
        compiler_params=pltpu.CompilerParams(vmem_limit_bytes=40 * 2**20),
        cost_estimate=pl.CostEstimate(flops=2 * 10**9, bytes_accessed=9 * 10**6, transcendentals=0),
        name="step_one",
    )(place, rows, diff, label, ao, occ, vir, occ_e, vir_e)


POS = {0: 0, 1: 1, -1: 2, 2: 3, -2: 4, 3: 5, -3: 6, 4: 7, -4: 7}
STAGES = ((0, 240), (240, 400), (400, 640))


def pair_kernel(
    lr_ref, base_ref, occr_ref, out_ref, rbuf, lbuf, lt_hi, lt_lo, ybuf,
    par_send, par_recv, hop_send, hop_recv, sib_send, sib_recv, l_send, l_recv, own_sem,
):
    pb, aux = lax.axis_index("pb"), lax.axis_index("aux")
    z, c = aux // 2, aux % 2
    partner = pb + 1 - 2 * (pb % 2)
    sibling = aux + 1 - 2 * c

    def at_z(dz, core):
        return lax.rem(z + dz + 8, 8) * 2 + core

    barrier = pltpu.get_barrier_semaphore()
    for far in range(1, 16):
        pl.semaphore_signal(barrier, inc=1, device_id={"aux": lax.rem(aux + far, 16)}, device_id_type=MESH)
    pl.semaphore_signal(barrier, inc=1, device_id={"pb": partner}, device_id_type=MESH)
    pl.semaphore_wait(barrier, 16)

    def place(pos, core):
        return pl.ds(pl.multiple_of(pos * 80 + core * 40, 8), 40)

    def chunk(pos, t):
        return rbuf.at[pl.ds(16 * t, 16), place(pos, c), :]

    def partner_copy(t):
        return pltpu.make_async_remote_copy(
            lr_ref.at[2 + t], chunk(0, t), par_send.at[t], par_recv.at[t],
            device_id={"pb": partner}, device_id_type=MESH,
        )

    def hop_copy(way, d, t):
        step = 1 - 2 * way
        return pltpu.make_async_remote_copy(
            chunk(POS[-step * (d - 1)], t), chunk(POS[-step * d], t),
            hop_send.at[way, d - 1, t], hop_recv.at[way, d - 1, t],
            device_id={"aux": at_z(step, c)}, device_id_type=MESH,
        )

    def sibling_copy(pos, t):
        return pltpu.make_async_remote_copy(
            chunk(pos, t), chunk(pos, t), sib_send.at[pos, t], sib_recv.at[pos, t],
            device_id={"aux": sibling}, device_id_type=MESH,
        )

    def row_copy(dz, cross):
        core = c + cross * (1 - 2 * c)
        to = at_z(dz, core)
        pos = POS[-dz]
        src, dst = lr_ref.at[pl.ds(0, 2), to], lbuf.at[:, place(pos, c), :]
        if dz == 0 and cross == 0:
            return pltpu.make_async_copy(src, dst, own_sem)
        return pltpu.make_async_remote_copy(
            src, dst, l_send.at[pos, cross], l_recv.at[pos, cross],
            device_id={"aux": to}, device_id_type=MESH,
        )

    def has_hop(way, d, t):
        return d < 4 or t == way

    partners = [partner_copy(t) for t in range(2)]
    for copy in partners:
        copy.start()
    rows = {(dz, cross): row_copy(dz, cross) for dz in (4, 3, -3, 2, -2, 1, -1, 0) for cross in range(2)}
    for copy in rows.values():
        copy.start()

    sent = []

    def send(copy):
        copy.start()
        sent.append(copy)

    for t in range(2):
        partners[t].wait_recv()
        for way in range(2):
            send(hop_copy(way, 1, t))
        send(sibling_copy(0, t))

    def relay(d):
        for t in range(2):
            for way in range(2):
                if not has_hop(way, d, t):
                    continue
                hop_copy(way, d, t).wait_recv()
                if d < 4 and has_hop(way, d + 1, t):
                    send(hop_copy(way, d + 1, t))
                send(sibling_copy(POS[-d if way == 0 else d], t))

    def left_sides():
        for (dz, cross), copy in rows.items():
            if dz == 0 and cross == 0:
                copy.wait()
            else:
                copy.wait_recv()
        for n, (first, last) in enumerate(STAGES):
            for s in range(2):
                part = lbuf[s, first:last, :]
                part = jnp.concatenate([part, jnp.zeros((256 - (last - first), 128), F32)], 0)
                hi, lo = halves(part.T)
                lt_hi[n, 128 * s : 128 * s + 128, :] = hi
                lt_lo[n, 128 * s : 128 * s + 128, :] = lo

    low = lax.broadcasted_iota(jnp.int32, (32, 128), 1) < 64

    def finish(n):
        t, j = n // 16, n % 16
        for s in range(2):
            def half(part, odd):
                return ybuf[n, pl.ds(128 * s + 64 * part + odd, 32, stride=2), :]

            re_e, re_d, im_e, im_d = half(0, 0), half(0, 1), half(1, 0), half(1, 1)
            inverse = 1.0 / (base_ref[2 * s + t] + occr_ref[t, pl.ds(j, 1), :])
            real = jnp.where(low, re_e, swap_sides(re_d)) - jnp.where(low, swap_sides(im_e), im_d)
            imag = jnp.where(low, swap_sides(re_e), re_d) + jnp.where(low, im_e, swap_sides(im_d))
            for part, value in enumerate((real, imag)):
                first = ((part * 2 + s) * 2 + t) * 512 + (j // 8) * 256 + j % 8
                out_ref[pl.ds(first, 32, stride=8), :] = value * inverse

    def multiply(stage):
        first, last = STAGES[stage]
        width = last - first

        def body(pair, _):
            r = jnp.concatenate([rbuf[pair * 2 + h, first:last, :] for h in range(2)], 1)
            hi, lo = halves(r)
            lh, ll = lt_hi[stage, :, :width], lt_lo[stage, :, :width]
            y = dot(lh, hi) + dot(ll, hi) + dot(lh, lo)
            for h in range(2):
                value = y[:, 128 * h : 128 * h + 128]
                if stage > 0:
                    value = value + ybuf[pair * 2 + h]
                ybuf[pair * 2 + h] = value
                if stage == 2:
                    finish(pair * 2 + h)
            return 0

        lax.fori_loop(0, 16, body, 0)

    def from_sibling(*positions):
        for pos in positions:
            for t in range(2):
                sibling_copy(pos, t).wait_recv()

    relay(1)
    left_sides()
    from_sibling(0, 1, 2)
    relay(2)
    multiply(0)
    relay(3)
    from_sibling(3, 4)
    multiply(1)
    relay(4)
    from_sibling(5, 6, 7)
    multiply(2)
    for copy in partners + sent:
        copy.wait_send()
    for (dz, cross), copy in rows.items():
        if dz != 0 or cross != 0:
            copy.wait_send()


def pair_sums(lr, base, occr):
    vmem = pl.BlockSpec(memory_space=pltpu.VMEM)
    dma = pltpu.SemaphoreType.DMA
    return pl.pallas_call(
        pair_kernel,
        out_shape=jax.ShapeDtypeStruct((4096, 128), F32),
        in_specs=[pl.BlockSpec(memory_space=pl.ANY), vmem, vmem],
        out_specs=vmem,
        scratch_shapes=[
            pltpu.VMEM((32, 640, 128), F32),
            pltpu.VMEM((2, 640, 128), F32),
            pltpu.VMEM((3, 256, 256), BF16),
            pltpu.VMEM((3, 256, 256), BF16),
            pltpu.VMEM((32, 256, 128), F32),
            dma((2,)), dma((2,)),
            dma((2, 4, 2)), dma((2, 4, 2)),
            dma((8, 2)), dma((8, 2)),
            dma((8, 2)), dma((8, 2)),
            dma,
        ],
        compiler_params=pltpu.CompilerParams(
            collective_id=0, has_side_effects=True, vmem_limit_bytes=48 * 2**20
        ),
        cost_estimate=pl.CostEstimate(flops=4 * 10**9, bytes_accessed=4 * 10**6, transcendentals=0),
        name="pair_sums",
    )(lr, base, occr)


def per_device(
    ao_blocks, occ_coef, vir_coef, occ_energy, vir_energy, kpoint_diff, transfer_label, chosen_rows
):
    place = jnp.stack([lax.axis_index("pb"), lax.axis_index("aux")]).astype(jnp.int32)
    ao = with_layout_constraint(
        ao_blocks.reshape(4, 40, 2, 50, 128), Layout(major_to_minor=(0, 1, 3, 2, 4))
    )
    ao = ao.transpose(0, 1, 3, 2, 4).reshape(4, 4000, 128)
    lr, base, occr = step_one(
        place, chosen_rows, kpoint_diff, transfer_label, ao,
        occ_coef.swapaxes(2, 3), vir_coef.swapaxes(2, 3), occ_energy, vir_energy,
    )
    out = pair_sums(lr.reshape(4, 16, 40, 128), base, occr)
    out = out.reshape(2, 2, 2, 2, 32, 8, 128).transpose(0, 1, 2, 3, 5, 4, 6)
    return out.reshape(1, 2, 2, 2, 1, 16, 4096)


def solution(mesh):
    in_specs = (P("pb", None, "aux", None, None), P(), P(), P(), P(), P(), P(), P())
    out_specs = P("pb", None, None, None, "aux", None, None)
    return jax.shard_map(
        per_device, mesh=mesh, in_specs=in_specs, out_specs=out_specs, check_vma=False
    )
```

```python
import functools

import jax
import jax.numpy as jnp
from jax import lax
from jax.experimental import pallas as pl
from jax.experimental.layout import Layout, with_layout_constraint
from jax.experimental.pallas import tpu as pltpu
from jax.sharding import PartitionSpec as P

MESH = pl.DeviceIdType.MESH
F32 = jnp.float32
BF16 = jnp.bfloat16

TILES = tuple(
    tuple((m, 80 * m - 128 * k) for m in range(8) if -80 < 80 * m - 128 * k < 128)
    for k in range(5)
)


def halves(x):
    hi = x.astype(BF16)
    return hi, (x - hi.astype(F32)).astype(BF16)


def dot(x, y):
    return jnp.dot(x, y, preferred_element_type=F32)


def swap_sides(x):
    return pltpu.roll(x, 64, 1)


def fill_weights(vir_ref, s, w_hi, w_lo):
    vre, vim = vir_ref[s, 0], vir_ref[s, 1]
    pad = jnp.zeros((128, 48), F32)
    for part, top, bottom in ((0, vre, vim), (1, -vim, vre)):
        stacked = jnp.concatenate([jnp.concatenate([top, bottom], 0), pad], 1)
        hi, lo = halves(stacked.T[:80])
        for k, blocks in enumerate(TILES):
            for b, (_, start) in enumerate(blocks):
                first, last = max(start, 0), min(start + 80, 128)
                to = (k, slice(part * 128 + first, part * 128 + last), slice(128 * b, 128 * b + 128))
                w_hi[to] = hi[first - start : last - start]
                w_lo[to] = lo[first - start : last - start]


def orbitals(s, ao_ref, occ_ref, vir_ref, put, w_hi, w_lo, x_hi, x_lo, t1):
    fill_weights(vir_ref, s, w_hi, w_lo)

    def load(pair, _):
        for k in range(5):
            sides = []
            for part in range(2):
                sides.append(
                    jnp.concatenate(
                        [
                            ao_ref[s, pl.ds(((pair * 2 + h) * 5 + k) * 2 + part, 40, stride=100), :]
                            for h in range(2)
                        ],
                        0,
                    )
                )
            hi, lo = halves(jnp.concatenate(sides, 1))
            at = pl.ds(pl.multiple_of(pair * 80, 16), 80)
            x_hi[k, at, :] = hi
            x_lo[k, at, :] = lo
        return 0

    lax.fori_loop(0, 5, load, 0)
    carry = None
    for k, blocks in enumerate(TILES):
        width = 128 * len(blocks)
        wh, wl = w_hi[k, :, :width], w_lo[k, :, :width]
        xh, xl = x_hi[k], x_lo[k]
        y = dot(xh, wh) + dot(xh, wl) + dot(xl, wh)
        for b, (m, start) in enumerate(blocks):
            value = y[:, 128 * b : 128 * b + 128]
            if start < 0:
                value = value + carry
            if start + 80 > 128:
                carry = value
                continue
            for g in range(10):
                t1[pl.ds(8 * g + m, 40, stride=80), :] = value[40 * g : 40 * g + 40]

    occ = jnp.concatenate([occ_ref[s, 0], occ_ref[s, 1]], 0)
    c_hi, c_lo = halves(occ)
    c_both = jnp.concatenate([c_hi, c_lo], 0)
    sign = jnp.where(lax.broadcasted_iota(jnp.int32, (16, 128), 1) < 64, 1.0, -1.0).astype(F32)

    def second(pair, _):
        rows = t1[pl.ds(pl.multiple_of(pair * 160, 8), 160), :]
        hi, lo = halves(jnp.concatenate([rows[:80], rows[80:]], 1))
        both = dot(c_both, hi)
        u = both[:32] + both[32:] + dot(c_hi, lo)
        for h in range(2):
            ure, uim = u[:16, 128 * h : 128 * h + 128], u[16:, 128 * h : 128 * h + 128]
            put(pair * 2 + h, ure + sign * swap_sides(uim))
        return 0

    lax.fori_loop(0, 20, second, 0, unroll=4)


def select_kernel(
    place, rows, diff, label, occ_ref, vir_ref, occ_e, vir_e, occ_out, vir_out, base_ref, occr_ref
):
    s = pl.program_id(0)
    occ_out[s] = occ_ref[0]
    vir_out[s] = vir_ref[0]

    @pl.when(s == 0)
    def _():
        slot, i = place[0], place[1]
        other = slot + 1 - 2 * (slot % 2)
        col = lax.broadcasted_iota(jnp.int32, (32, 64), 1)
        row = lax.broadcasted_iota(jnp.int32, (32, 64), 0)
        low = lax.broadcasted_iota(jnp.int32, (32, 128), 1) < 64
        lane = lax.broadcasted_iota(jnp.int32, (1, 16), 1)
        eye = lax.broadcasted_iota(jnp.int32, (16, 16), 0) == lax.broadcasted_iota(jnp.int32, (16, 16), 1)
        for b in range(2):
            ki = rows[slot, b]
            ka = diff[ki, label[slot]]
            occ_left = jnp.sum(jnp.where(lane == i, occ_e[pl.ds(ki, 1), :], 0.0), axis=1, keepdims=True)
            line = vir_e[pl.ds(ka, 1), :]
            even = jnp.sum(jnp.where(col == 2 * row, line, 0.0), axis=1, keepdims=True)
            odd = jnp.sum(jnp.where(col == 2 * row + 1, line, 0.0), axis=1, keepdims=True)
            left = occ_left - jnp.where(low, even, odd)
            for t in range(2):
                kj = rows[other, 2 + t]
                kb = diff[kj, label[other]]
                right = vir_e[pl.ds(kb, 1), :]
                base_ref[2 * b + t] = left - jnp.concatenate([right, right], 1)
                if b == 0:
                    occ_right = jnp.sum(jnp.where(eye, occ_e[pl.ds(kj, 1), :], 0.0), axis=1, keepdims=True)
                    occr_ref[t] = jnp.broadcast_to(occ_right, (16, 128))


def select(place, rows, diff, label, occ, vir, occ_e, vir_e):
    def occ_at(s, place, rows, diff, label):
        return (rows[place[0], s], 0, 0, 0)

    def vir_at(s, place, rows, diff, label):
        return (diff[rows[place[0], s], label[place[0]]], 0, 0, 0)

    def whole(*shape):
        return pl.BlockSpec(shape, lambda s, *_: (0,) * len(shape))

    shapes = ((4, 2, 16, 80), (4, 2, 64, 80), (4, 32, 128), (2, 16, 128))
    return pl.pallas_call(
        select_kernel,
        out_shape=tuple(jax.ShapeDtypeStruct(shape, F32) for shape in shapes),
        grid_spec=pltpu.PrefetchScalarGridSpec(
            num_scalar_prefetch=4,
            grid=(4,),
            in_specs=[
                pl.BlockSpec((1, 2, 16, 80), occ_at),
                pl.BlockSpec((1, 2, 64, 80), vir_at),
                whole(27, 16),
                whole(27, 64),
            ],
            out_specs=tuple(whole(*shape) for shape in shapes),
        ),
        compiler_params=pltpu.CompilerParams(vmem_limit_bytes=48 * 2**20),
        name="select",
    )(place, rows, diff, label, occ, vir, occ_e, vir_e)


POS = {0: 0, 1: 1, -1: 2, 2: 3, -2: 4, 3: 5, -3: 6, 4: 7, -4: 7}
STAGES = ((0, 240), (240, 400), (400, 640))
CHUNKS = 4
LINES = 32 // CHUNKS


def pair_kernel(
    ao_hbm, occ_ref, vir_ref, base_ref, occr_ref, out_ref,
    ao_ref, w_hi, w_lo, x_hi, x_lo, t1, lr_ref, rbuf, lbuf, lt_hi, lt_lo, ybuf,
    ao_sem, par_send, par_recv, hop_send, hop_recv, sib_send, sib_recv, l_send, l_recv, own_sem,
):
    pb, aux = lax.axis_index("pb"), lax.axis_index("aux")
    z, c = aux // 2, aux % 2
    partner = pb + 1 - 2 * (pb % 2)
    sibling = aux + 1 - 2 * c

    def at_z(dz, core):
        return lax.rem(z + dz + 8, 8) * 2 + core

    barrier = pltpu.get_barrier_semaphore()
    for far in range(1, 16):
        pl.semaphore_signal(barrier, inc=1, device_id={"aux": lax.rem(aux + far, 16)}, device_id_type=MESH)
    pl.semaphore_signal(barrier, inc=1, device_id={"pb": partner}, device_id_type=MESH)

    blocks = {s: pltpu.make_async_copy(ao_hbm.at[s], ao_ref.at[s], ao_sem.at[s]) for s in (0, 2, 1, 3)}
    for copy in blocks.values():
        copy.start()
    w_hi[...] = jnp.zeros_like(w_hi)
    w_lo[...] = jnp.zeros_like(w_lo)

    def make(s):
        blocks[s].wait()

        def put(p, value):
            lr_ref.reshape(2560, 128)[pl.ds(s * 640 + p, 16, stride=40), :] = value

        orbitals(s, ao_ref, occ_ref, vir_ref, put, w_hi, w_lo, x_hi, x_lo, t1)

    def place(pos, core):
        return pl.ds(pl.multiple_of(pos * 80 + core * 40, 8), 40)

    def chunk(pos, q):
        return rbuf.at[pl.ds(LINES * q, LINES), place(pos, c), :]

    def partner_copy(q):
        return pltpu.make_async_remote_copy(
            lr_ref.at[pl.ds(32 + LINES * q, LINES)], chunk(0, q), par_send.at[q], par_recv.at[q],
            device_id={"pb": partner}, device_id_type=MESH,
        )

    def hop_copy(way, d, q):
        step = 1 - 2 * way
        return pltpu.make_async_remote_copy(
            chunk(POS[-step * (d - 1)], q), chunk(POS[-step * d], q),
            hop_send.at[way, d - 1, q], hop_recv.at[way, d - 1, q],
            device_id={"aux": at_z(step, c)}, device_id_type=MESH,
        )

    def sibling_copy(pos, q):
        return pltpu.make_async_remote_copy(
            chunk(pos, q), chunk(pos, q), sib_send.at[pos, q], sib_recv.at[pos, q],
            device_id={"aux": sibling}, device_id_type=MESH,
        )

    def row_copy(s, dz, cross):
        core = c + cross * (1 - 2 * c)
        to = at_z(dz, core)
        pos = POS[-dz]
        src, dst = lr_ref.at[16 * s + to], lbuf.at[s, place(pos, c), :]
        if dz == 0 and cross == 0:
            return pltpu.make_async_copy(src, dst, own_sem.at[s])
        return pltpu.make_async_remote_copy(
            src, dst, l_send.at[s, pos, cross], l_recv.at[s, pos, cross],
            device_id={"aux": to}, device_id_type=MESH,
        )

    rows = {
        (s, dz, cross): row_copy(s, dz, cross)
        for s in range(2) for dz in (4, 3, -3, 2, -2, 1, -1, 0) for cross in range(2)
    }
    partners = [partner_copy(q) for q in range(CHUNKS)]
    sent = []

    def send(copy):
        copy.start()
        sent.append(copy)

    def send_rows(s):
        for (block, _, _), copy in rows.items():
            if block == s:
                copy.start()

    def send_partner(t):
        for q in range(CHUNKS):
            if q * LINES // 16 == t:
                partners[q].start()

    def has_hop(way, d, q):
        return d < 4 or q * LINES // 16 == way

    def relay(d, q):
        for way in range(2):
            if not has_hop(way, d, q):
                continue
            hop_copy(way, d, q).wait_recv()
            if d < 4 and has_hop(way, d + 1, q):
                send(hop_copy(way, d + 1, q))
            send(sibling_copy(POS[-d if way == 0 else d], q))

    def left_sides():
        for (s, dz, cross), copy in rows.items():
            if dz == 0 and cross == 0:
                copy.wait()
            else:
                copy.wait_recv()
        for n, (first, last) in enumerate(STAGES):
            for s in range(2):
                part = lbuf[s, first:last, :]
                part = jnp.concatenate([part, jnp.zeros((256 - (last - first), 128), F32)], 0)
                hi, lo = halves(part.T)
                lt_hi[n, 128 * s : 128 * s + 128, :] = hi
                lt_lo[n, 128 * s : 128 * s + 128, :] = lo

    low = lax.broadcasted_iota(jnp.int32, (32, 128), 1) < 64

    def finish(n):
        t, j = n // 16, n % 16
        for s in range(2):
            def half(part, odd):
                return ybuf[n, pl.ds(128 * s + 64 * part + odd, 32, stride=2), :]

            re_e, re_d, im_e, im_d = half(0, 0), half(0, 1), half(1, 0), half(1, 1)
            inverse = 1.0 / (base_ref[2 * s + t] + occr_ref[t, pl.ds(j, 1), :])
            real = jnp.where(low, re_e, swap_sides(re_d)) - jnp.where(low, swap_sides(im_e), im_d)
            imag = jnp.where(low, swap_sides(re_e), re_d) + jnp.where(low, im_e, swap_sides(im_d))
            for part, value in enumerate((real, imag)):
                first = ((part * 2 + s) * 2 + t) * 512 + (j // 8) * 256 + j % 8
                out_ref[pl.ds(first, 32, stride=8), :] = value * inverse

    def multiply(stage, q):
        first, last = STAGES[stage]
        width = last - first

        def body(pair, _):
            n = LINES * q + pair * 2
            r = jnp.concatenate([rbuf[n + h, first:last, :] for h in range(2)], 1)
            hi, lo = halves(r)
            lh, ll = lt_hi[stage, :, :width], lt_lo[stage, :, :width]
            y = dot(lh, hi) + dot(ll, hi) + dot(lh, lo)
            for h in range(2):
                value = y[:, 128 * h : 128 * h + 128]
                if stage > 0:
                    value = value + ybuf[n + h]
                ybuf[n + h] = value
                if stage == 2:
                    finish(n + h)
            return 0

        lax.fori_loop(0, LINES // 2, body, 0)

    def from_sibling(q, *positions):
        for pos in positions:
            sibling_copy(pos, q).wait_recv()

    def open_ring(q):
        partners[q].wait_recv()
        for way in range(2):
            send(hop_copy(way, 1, q))
        send(sibling_copy(0, q))

    make(0)
    pl.semaphore_wait(barrier, 16)
    send_rows(0)
    make(2)
    send_partner(0)
    make(1)
    send_rows(1)
    make(3)
    send_partner(1)
    for q in range(CHUNKS):
        open_ring(q)
    for q in range(CHUNKS):
        relay(1, q)
    left_sides()
    for q in range(CHUNKS):
        relay(2, q)
        from_sibling(q, 0, 1, 2)
        multiply(0, q)
    for q in range(CHUNKS):
        relay(3, q)
        from_sibling(q, 3, 4)
        multiply(1, q)
    for half in range(CHUNKS // 2):
        for q in (half, half + CHUNKS // 2):
            relay(4, q)
        for q in (half, half + CHUNKS // 2):
            from_sibling(q, 5, 6, 7)
            multiply(2, q)
    for copy in partners + sent:
        copy.wait_send()
    for (s, dz, cross), copy in rows.items():
        if dz != 0 or cross != 0:
            copy.wait_send()


def pair_sums(ao, occ, vir, base, occr):
    vmem = pl.BlockSpec(memory_space=pltpu.VMEM)
    dma = pltpu.SemaphoreType.DMA
    return pl.pallas_call(
        pair_kernel,
        out_shape=jax.ShapeDtypeStruct((4096, 128), F32),
        in_specs=[pl.BlockSpec(memory_space=pl.ANY), vmem, vmem, vmem, vmem],
        out_specs=vmem,
        scratch_shapes=[
            pltpu.VMEM((4, 4000, 128), F32),
            pltpu.VMEM((5, 256, 384), BF16),
            pltpu.VMEM((5, 256, 384), BF16),
            pltpu.VMEM((5, 400, 256), BF16),
            pltpu.VMEM((5, 400, 256), BF16),
            pltpu.VMEM((3200, 128), F32),
            pltpu.VMEM((64, 40, 128), F32),
            pltpu.VMEM((32, 640, 128), F32),
            pltpu.VMEM((2, 640, 128), F32),
            pltpu.VMEM((3, 256, 256), BF16),
            pltpu.VMEM((3, 256, 256), BF16),
            pltpu.VMEM((32, 256, 128), F32),
            dma((4,)),
            dma((CHUNKS,)), dma((CHUNKS,)),
            dma((2, 4, CHUNKS)), dma((2, 4, CHUNKS)),
            dma((8, CHUNKS)), dma((8, CHUNKS)),
            dma((2, 8, 2)), dma((2, 8, 2)),
            dma((2,)),
        ],
        compiler_params=pltpu.CompilerParams(
            collective_id=0, has_side_effects=True, vmem_limit_bytes=48 * 2**20
        ),
        cost_estimate=pl.CostEstimate(flops=6 * 10**9, bytes_accessed=12 * 10**6, transcendentals=0),
        name="pair_sums",
    )(ao, occ, vir, base, occr)


def per_device(
    ao_blocks, occ_coef, vir_coef, occ_energy, vir_energy, kpoint_diff, transfer_label, chosen_rows
):
    place = jnp.stack([lax.axis_index("pb"), lax.axis_index("aux")]).astype(jnp.int32)
    ao = with_layout_constraint(
        ao_blocks.reshape(4, 40, 2, 50, 128), Layout(major_to_minor=(0, 1, 3, 2, 4))
    )
    ao = ao.transpose(0, 1, 3, 2, 4).reshape(4, 4000, 128)
    occ, vir, base, occr = select(
        place, chosen_rows, kpoint_diff, transfer_label,
        occ_coef.swapaxes(2, 3), vir_coef.swapaxes(2, 3), occ_energy, vir_energy,
    )
    out = pair_sums(ao, occ, vir, base, occr)
    out = out.reshape(2, 2, 2, 2, 32, 8, 128).transpose(0, 1, 2, 3, 5, 4, 6)
    return out.reshape(1, 2, 2, 2, 1, 16, 4096)


def solution(mesh):
    in_specs = (P("pb", None, "aux", None, None), P(), P(), P(), P(), P(), P(), P())
    out_specs = P("pb", None, None, None, "aux", None, None)
    return jax.shard_map(
        per_device, mesh=mesh, in_specs=in_specs, out_specs=out_specs, check_vma=False
    )
```

```python
import jax
import jax.numpy as jnp
from jax import lax
from jax.experimental import pallas as pl
from jax.experimental.layout import Layout, with_layout_constraint
from jax.experimental.pallas import tpu as pltpu
from jax.sharding import PartitionSpec as P

MESH = pl.DeviceIdType.MESH
F32 = jnp.float32
BF16 = jnp.bfloat16

TILES = tuple(
    tuple((m, 80 * m - 128 * k) for m in range(8) if -80 < 80 * m - 128 * k < 128)
    for k in range(5)
)


def halves(x):
    hi = x.astype(BF16)
    return hi, (x - hi.astype(F32)).astype(BF16)


def dot(x, y):
    return jnp.dot(x, y, preferred_element_type=F32)


def swap_sides(x):
    return pltpu.roll(x, 64, 1)


def fill_weights(vre, vim, w_hi, w_lo):
    pad = jnp.zeros((128, 48), F32)
    for part, top, bottom in ((0, vre, vim), (1, -vim, vre)):
        stacked = jnp.concatenate([jnp.concatenate([top, bottom], 0), pad], 1)
        hi, lo = halves(stacked.T[:80])
        for k, blocks in enumerate(TILES):
            for b, (_, start) in enumerate(blocks):
                first, last = max(start, 0), min(start + 80, 128)
                to = (k, slice(part * 128 + first, part * 128 + last), slice(128 * b, 128 * b + 128))
                w_hi[to] = hi[first - start : last - start]
                w_lo[to] = lo[first - start : last - start]


def orbitals(s, ao_ref, occ, vre, vim, put, w_hi, w_lo, x_hi, x_lo, t1):
    fill_weights(vre, vim, w_hi, w_lo)

    def load(pair, _):
        for k in range(5):
            sides = []
            for part in range(2):
                sides.append(
                    jnp.concatenate(
                        [
                            ao_ref[s, pl.ds(((pair * 2 + h) * 5 + k) * 2 + part, 40, stride=100), :]
                            for h in range(2)
                        ],
                        0,
                    )
                )
            hi, lo = halves(jnp.concatenate(sides, 1))
            at = pl.ds(pl.multiple_of(pair * 80, 16), 80)
            x_hi[k, at, :] = hi
            x_lo[k, at, :] = lo
        return 0

    lax.fori_loop(0, 5, load, 0)
    carry = None
    for k, blocks in enumerate(TILES):
        width = 128 * len(blocks)
        wh, wl = w_hi[k, :, :width], w_lo[k, :, :width]
        xh, xl = x_hi[k], x_lo[k]
        y = dot(xh, wh) + dot(xh, wl) + dot(xl, wh)
        for b, (m, start) in enumerate(blocks):
            value = y[:, 128 * b : 128 * b + 128]
            if start < 0:
                value = value + carry
            if start + 80 > 128:
                carry = value
                continue
            for g in range(10):
                t1[pl.ds(8 * g + m, 40, stride=80), :] = value[40 * g : 40 * g + 40]

    c_hi, c_lo = halves(occ)
    c_both = jnp.concatenate([c_hi, c_lo], 0)
    sign = jnp.where(lax.broadcasted_iota(jnp.int32, (16, 128), 1) < 64, 1.0, -1.0).astype(F32)

    def second(pair, _):
        rows = t1[pl.ds(pl.multiple_of(pair * 160, 8), 160), :]
        hi, lo = halves(jnp.concatenate([rows[:80], rows[80:]], 1))
        both = dot(c_both, hi)
        u = both[:32] + both[32:] + dot(c_hi, lo)
        for h in range(2):
            ure, uim = u[:16, 128 * h : 128 * h + 128], u[16:, 128 * h : 128 * h + 128]
            put(pair * 2 + h, ure + sign * swap_sides(uim))
        return 0

    lax.fori_loop(0, 20, second, 0, unroll=4)


POS = {0: 0, 1: 1, -1: 2, 2: 3, -2: 4, 3: 5, -3: 6, 4: 7, -4: 7}
STAGES = ((0, 240), (240, 400), (400, 640))
CHUNKS = 4
LINES = 32 // CHUNKS


def pair_kernel(
    ao_hbm, occ_hbm, vir_hbm, occ_e_hbm, vir_e_hbm, diff_hbm, label_hbm, rows_hbm, out_ref,
    occ_ref, vir_ref, occ_e, vir_e, diff, label, chosen, base_ref, occr_ref, ao_ref, w_hi, w_lo, x_hi, x_lo, t1, lr_ref, rbuf, lbuf, lt_hi, lt_lo, ybuf,
    in_sem, ao_sem, par_send, par_recv, hop_send, hop_recv, sib_send, sib_recv, l_send, l_recv, own_sem,
):
    pb, aux = lax.axis_index("pb"), lax.axis_index("aux")
    z, c = aux // 2, aux % 2
    partner = pb + 1 - 2 * (pb % 2)
    sibling = aux + 1 - 2 * c

    def at_z(dz, core):
        return lax.rem(z + dz + 8, 8) * 2 + core

    barrier = pltpu.get_barrier_semaphore()
    for far in range(1, 16):
        pl.semaphore_signal(barrier, inc=1, device_id={"aux": lax.rem(aux + far, 16)}, device_id_type=MESH)
    pl.semaphore_signal(barrier, inc=1, device_id={"pb": partner}, device_id_type=MESH)

    inputs = [
        pltpu.make_async_copy(src, dst, in_sem.at[n])
        for n, (src, dst) in enumerate(
            (
                (rows_hbm, chosen), (diff_hbm, diff), (label_hbm, label), (vir_hbm, vir_ref),
                (occ_hbm, occ_ref), (occ_e_hbm, occ_e), (vir_e_hbm, vir_e),
            )
        )
    ]
    for copy in inputs:
        copy.start()
    blocks = {s: pltpu.make_async_copy(ao_hbm.at[s], ao_ref.at[s], ao_sem.at[s]) for s in (0, 2, 1, 3)}
    for copy in blocks.values():
        copy.start()
    w_hi[...] = jnp.zeros_like(w_hi)
    w_lo[...] = jnp.zeros_like(w_lo)

    for copy in inputs:
        copy.wait()

    def energies():
        col = lax.broadcasted_iota(jnp.int32, (32, 64), 1)
        row = lax.broadcasted_iota(jnp.int32, (32, 64), 0)
        first_lanes = lax.broadcasted_iota(jnp.int32, (32, 128), 1) < 64

        def pick(values, k):
            lane = lax.broadcasted_iota(jnp.int32, values.shape, 1)
            return jnp.sum(jnp.where(lane == k, values, 0.0), axis=1, keepdims=True)

        for b in range(2):
            ki = chosen[b, pb]
            line = vir_e[pl.ds(diff[ki, label[pb]], 1), :]
            even = jnp.sum(jnp.where(col == 2 * row, line, 0.0), axis=1, keepdims=True)
            odd = jnp.sum(jnp.where(col == 2 * row + 1, line, 0.0), axis=1, keepdims=True)
            left = pick(occ_e[pl.ds(aux, 1), :], ki) - jnp.where(first_lanes, even, odd)
            for t in range(2):
                kj = chosen[2 + t, partner]
                right = vir_e[pl.ds(diff[kj, label[partner]], 1), :]
                base_ref[2 * b + t] = left - jnp.concatenate([right, right], 1)
                if b == 0:
                    occr_ref[t] = jnp.broadcast_to(pick(occ_e[...], kj), (16, 128))

    def make(s):
        blocks[s].wait()
        k = chosen[s, pb]
        ka = diff[k, label[pb]]
        occ = jnp.concatenate([occ_ref[k, 0], occ_ref[k, 1]], 0)

        def put(p, value):
            lr_ref.reshape(2560, 128)[pl.ds(s * 640 + p, 16, stride=40), :] = value

        orbitals(s, ao_ref, occ, vir_ref[ka, 0], vir_ref[ka, 1], put, w_hi, w_lo, x_hi, x_lo, t1)

    def place(pos, core):
        return pl.ds(pl.multiple_of(pos * 80 + core * 40, 8), 40)

    def chunk(pos, q):
        return rbuf.at[pl.ds(LINES * q, LINES), place(pos, c), :]

    def partner_copy(q):
        return pltpu.make_async_remote_copy(
            lr_ref.at[pl.ds(32 + LINES * q, LINES)], chunk(0, q), par_send.at[q], par_recv.at[q],
            device_id={"pb": partner}, device_id_type=MESH,
        )

    def hop_copy(way, d, q):
        step = 1 - 2 * way
        return pltpu.make_async_remote_copy(
            chunk(POS[-step * (d - 1)], q), chunk(POS[-step * d], q),
            hop_send.at[way, d - 1, q], hop_recv.at[way, d - 1, q],
            device_id={"aux": at_z(step, c)}, device_id_type=MESH,
        )

    def sibling_copy(pos, q):
        return pltpu.make_async_remote_copy(
            chunk(pos, q), chunk(pos, q), sib_send.at[pos, q], sib_recv.at[pos, q],
            device_id={"aux": sibling}, device_id_type=MESH,
        )

    def row_copy(s, dz, cross):
        core = c + cross * (1 - 2 * c)
        to = at_z(dz, core)
        pos = POS[-dz]
        src, dst = lr_ref.at[16 * s + to], lbuf.at[s, place(pos, c), :]
        if dz == 0 and cross == 0:
            return pltpu.make_async_copy(src, dst, own_sem.at[s])
        return pltpu.make_async_remote_copy(
            src, dst, l_send.at[s, pos, cross], l_recv.at[s, pos, cross],
            device_id={"aux": to}, device_id_type=MESH,
        )

    rows = {
        (s, dz, cross): row_copy(s, dz, cross)
        for s in range(2) for dz in (4, 3, -3, 2, -2, 1, -1, 0) for cross in range(2)
    }
    partners = [partner_copy(q) for q in range(CHUNKS)]
    sent = []

    def send(copy):
        copy.start()
        sent.append(copy)

    def send_rows(s):
        for (block, _, _), copy in rows.items():
            if block == s:
                copy.start()

    def send_partner(t):
        for q in range(CHUNKS):
            if q * LINES // 16 == t:
                partners[q].start()

    def has_hop(way, d, q):
        return d < 4 or q * LINES // 16 == way

    def relay(d, q):
        for way in range(2):
            if not has_hop(way, d, q):
                continue
            hop_copy(way, d, q).wait_recv()
            if d < 4 and has_hop(way, d + 1, q):
                send(hop_copy(way, d + 1, q))
            send(sibling_copy(POS[-d if way == 0 else d], q))

    def left_sides():
        for (s, dz, cross), copy in rows.items():
            if dz == 0 and cross == 0:
                copy.wait()
            else:
                copy.wait_recv()
        for n, (first, last) in enumerate(STAGES):
            for s in range(2):
                part = lbuf[s, first:last, :]
                part = jnp.concatenate([part, jnp.zeros((256 - (last - first), 128), F32)], 0)
                hi, lo = halves(part.T)
                lt_hi[n, 128 * s : 128 * s + 128, :] = hi
                lt_lo[n, 128 * s : 128 * s + 128, :] = lo

    low = lax.broadcasted_iota(jnp.int32, (32, 128), 1) < 64

    def finish(n):
        t, j = n // 16, n % 16
        for s in range(2):
            def half(part, odd):
                return ybuf[n, pl.ds(128 * s + 64 * part + odd, 32, stride=2), :]

            re_e, re_d, im_e, im_d = half(0, 0), half(0, 1), half(1, 0), half(1, 1)
            inverse = 1.0 / (base_ref[2 * s + t] + occr_ref[t, pl.ds(j, 1), :])
            real = jnp.where(low, re_e, swap_sides(re_d)) - jnp.where(low, swap_sides(im_e), im_d)
            imag = jnp.where(low, swap_sides(re_e), re_d) + jnp.where(low, im_e, swap_sides(im_d))
            for part, value in enumerate((real, imag)):
                first = ((part * 2 + s) * 2 + t) * 512 + (j // 8) * 256 + j % 8
                out_ref[pl.ds(first, 32, stride=8), :] = value * inverse

    def multiply(stage, q):
        first, last = STAGES[stage]
        width = last - first

        def body(pair, _):
            n = LINES * q + pair * 2
            r = jnp.concatenate([rbuf[n + h, first:last, :] for h in range(2)], 1)
            hi, lo = halves(r)
            lh, ll = lt_hi[stage, :, :width], lt_lo[stage, :, :width]
            y = dot(lh, hi) + dot(ll, hi) + dot(lh, lo)
            for h in range(2):
                value = y[:, 128 * h : 128 * h + 128]
                if stage > 0:
                    value = value + ybuf[n + h]
                ybuf[n + h] = value
                if stage == 2:
                    finish(n + h)
            return 0

        lax.fori_loop(0, LINES // 2, body, 0)

    def from_sibling(q, *positions):
        for pos in positions:
            sibling_copy(pos, q).wait_recv()

    def open_ring(q):
        partners[q].wait_recv()
        for way in range(2):
            send(hop_copy(way, 1, q))
        send(sibling_copy(0, q))

    make(0)
    pl.semaphore_wait(barrier, 16)
    send_rows(0)
    make(2)
    send_partner(0)
    energies()
    make(1)
    send_rows(1)
    make(3)
    send_partner(1)
    for q in range(CHUNKS):
        open_ring(q)
    for q in range(CHUNKS):
        relay(1, q)
    left_sides()
    for q in range(CHUNKS):
        relay(2, q)
        from_sibling(q, 0, 1, 2)
        multiply(0, q)
    for q in range(CHUNKS):
        relay(3, q)
        from_sibling(q, 3, 4)
        multiply(1, q)
    for half in range(CHUNKS // 2):
        for q in (half, half + CHUNKS // 2):
            relay(4, q)
        for q in (half, half + CHUNKS // 2):
            from_sibling(q, 5, 6, 7)
            multiply(2, q)
    for copy in partners + sent:
        copy.wait_send()
    for (s, dz, cross), copy in rows.items():
        if dz != 0 or cross != 0:
            copy.wait_send()


def pair_sums(*operands):
    dma = pltpu.SemaphoreType.DMA
    return pl.pallas_call(
        pair_kernel,
        out_shape=jax.ShapeDtypeStruct((4096, 128), F32),
        in_specs=[pl.BlockSpec(memory_space=pltpu.HBM)] * 8,
        out_specs=pl.BlockSpec(memory_space=pltpu.VMEM),
        scratch_shapes=[
            pltpu.VMEM((27, 2, 16, 80), F32),
            pltpu.VMEM((27, 2, 64, 80), F32),
            pltpu.VMEM((16, 27), F32),
            pltpu.VMEM((27, 64), F32),
            pltpu.SMEM((27, 27), jnp.int32),
            pltpu.SMEM((16,), jnp.int32),
            pltpu.SMEM((4, 16), jnp.int32),
            pltpu.VMEM((4, 32, 128), F32),
            pltpu.VMEM((2, 16, 128), F32),
            pltpu.VMEM((4, 4000, 128), F32),
            pltpu.VMEM((5, 256, 384), BF16),
            pltpu.VMEM((5, 256, 384), BF16),
            pltpu.VMEM((5, 400, 256), BF16),
            pltpu.VMEM((5, 400, 256), BF16),
            pltpu.VMEM((3200, 128), F32),
            pltpu.VMEM((64, 40, 128), F32),
            pltpu.VMEM((32, 640, 128), F32),
            pltpu.VMEM((2, 640, 128), F32),
            pltpu.VMEM((3, 256, 256), BF16),
            pltpu.VMEM((3, 256, 256), BF16),
            pltpu.VMEM((32, 256, 128), F32),
            dma((7,)),
            dma((4,)),
            dma((CHUNKS,)), dma((CHUNKS,)),
            dma((2, 4, CHUNKS)), dma((2, 4, CHUNKS)),
            dma((8, CHUNKS)), dma((8, CHUNKS)),
            dma((2, 8, 2)), dma((2, 8, 2)),
            dma((2,)),
        ],
        compiler_params=pltpu.CompilerParams(
            collective_id=0, has_side_effects=True, vmem_limit_bytes=56 * 2**20
        ),
        cost_estimate=pl.CostEstimate(flops=6 * 10**9, bytes_accessed=12 * 10**6, transcendentals=0),
        name="pair_sums",
    )(*operands)


def per_device(
    ao_blocks, occ_coef, vir_coef, occ_energy, vir_energy, kpoint_diff, transfer_label, chosen_rows
):
    ao = with_layout_constraint(
        ao_blocks.reshape(4, 40, 2, 50, 128), Layout(major_to_minor=(0, 1, 3, 2, 4))
    )
    ao = ao.transpose(0, 1, 3, 2, 4).reshape(4, 4000, 128)
    out = pair_sums(
        ao, occ_coef.swapaxes(2, 3), vir_coef.swapaxes(2, 3), occ_energy.T, vir_energy,
        kpoint_diff, transfer_label, chosen_rows.T,
    )
    out = out.reshape(2, 2, 2, 2, 32, 8, 128).transpose(0, 1, 2, 3, 5, 4, 6)
    return out.reshape(1, 2, 2, 2, 1, 16, 4096)


def solution(mesh):
    in_specs = (P("pb", None, "aux", None, None), P(), P(), P(), P(), P(), P(), P())
    out_specs = P("pb", None, None, None, "aux", None, None)
    return jax.shard_map(
        per_device, mesh=mesh, in_specs=in_specs, out_specs=out_specs, check_vma=False
    )
```

```python
import jax
import jax.numpy as jnp
from jax import lax
from jax.experimental import pallas as pl
from jax.experimental.layout import Layout, with_layout_constraint
from jax.experimental.pallas import tpu as pltpu
from jax.sharding import PartitionSpec as P

MESH = pl.DeviceIdType.MESH
F32 = jnp.float32
BF16 = jnp.bfloat16

TILES = tuple(
    tuple((m, 80 * m - 128 * k) for m in range(8) if -80 < 80 * m - 128 * k < 128)
    for k in range(5)
)


def halves(x):
    hi = x.astype(BF16)
    return hi, (x - hi.astype(F32)).astype(BF16)


def dot(x, y):
    return jnp.dot(x, y, preferred_element_type=F32)


def swap_sides(x):
    return pltpu.roll(x, 64, 1)


def fill_weights(vre, vim, w_hi, w_lo):
    pad = jnp.zeros((128, 48), F32)
    for part, top, bottom in ((0, vre, vim), (1, -vim, vre)):
        stacked = jnp.concatenate([jnp.concatenate([top, bottom], 0), pad], 1)
        hi, lo = halves(stacked.T[:80])
        for k, blocks in enumerate(TILES):
            for b, (_, start) in enumerate(blocks):
                first, last = max(start, 0), min(start + 80, 128)
                to = (k, slice(part * 128 + first, part * 128 + last), slice(128 * b, 128 * b + 128))
                w_hi[to] = hi[first - start : last - start]
                w_lo[to] = lo[first - start : last - start]


def orbitals(s, ao_ref, occ, vre, vim, put, w_hi, w_lo, x_hi, x_lo, t1):
    fill_weights(vre, vim, w_hi, w_lo)

    def load(pair, _):
        for k in range(5):
            sides = []
            for part in range(2):
                sides.append(
                    jnp.concatenate(
                        [
                            ao_ref[s, pl.ds(((pair * 2 + h) * 5 + k) * 2 + part, 40, stride=100), :]
                            for h in range(2)
                        ],
                        0,
                    )
                )
            hi, lo = halves(jnp.concatenate(sides, 1))
            at = pl.ds(pl.multiple_of(pair * 80, 16), 80)
            x_hi[k, at, :] = hi
            x_lo[k, at, :] = lo
        return 0

    lax.fori_loop(0, 5, load, 0, unroll=5)
    carry = None
    for k, blocks in enumerate(TILES):
        width = 128 * len(blocks)
        wh, wl = w_hi[k, :, :width], w_lo[k, :, :width]
        xh, xl = x_hi[k], x_lo[k]
        y = dot(xh, wh) + dot(xh, wl) + dot(xl, wh)
        for b, (m, start) in enumerate(blocks):
            value = y[:, 128 * b : 128 * b + 128]
            if start < 0:
                value = value + carry
            if start + 80 > 128:
                carry = value
                continue
            for g in range(10):
                t1[pl.ds(8 * g + m, 40, stride=80), :] = value[40 * g : 40 * g + 40]

    c_hi, c_lo = halves(occ)
    c_both = jnp.concatenate([c_hi, c_lo], 0)
    sign = jnp.where(lax.broadcasted_iota(jnp.int32, (16, 128), 1) < 64, 1.0, -1.0).astype(F32)

    def second(pair, _):
        rows = t1[pl.ds(pl.multiple_of(pair * 160, 8), 160), :]
        hi, lo = halves(jnp.concatenate([rows[:80], rows[80:]], 1))
        both = dot(c_both, hi)
        u = both[:32] + both[32:] + dot(c_hi, lo)
        for h in range(2):
            ure, uim = u[:16, 128 * h : 128 * h + 128], u[16:, 128 * h : 128 * h + 128]
            put(pair * 2 + h, ure + sign * swap_sides(uim))
        return 0

    lax.fori_loop(0, 20, second, 0, unroll=10)


POS = {0: 0, 1: 1, -1: 2, 2: 3, -2: 4, 3: 5, -3: 6, 4: 7, -4: 7}
STAGES = ((0, 240), (240, 400), (400, 640))
CHUNKS = 4
LINES = 32 // CHUNKS


def pair_kernel(
    ao_hbm, occ_hbm, vir_hbm, occ_e_hbm, vir_e_hbm, diff_hbm, label_hbm, rows_hbm, out_ref,
    occ_ref, vir_ref, occ_e, vir_e, diff, label, chosen, base_ref, occr_ref, ao_ref, w_hi, w_lo, x_hi, x_lo, t1, lr_ref, rbuf, lbuf, lt_hi, lt_lo, ybuf,
    in_sem, ao_sem, par_send, par_recv, hop_send, hop_recv, sib_send, sib_recv, l_send, l_recv, own_sem,
):
    pb, aux = lax.axis_index("pb"), lax.axis_index("aux")
    z, c = aux // 2, aux % 2
    partner = pb + 1 - 2 * (pb % 2)
    sibling = aux + 1 - 2 * c

    def at_z(dz, core):
        return lax.rem(z + dz + 8, 8) * 2 + core

    barrier = pltpu.get_barrier_semaphore()
    for far in range(1, 16):
        pl.semaphore_signal(barrier, inc=1, device_id={"aux": lax.rem(aux + far, 16)}, device_id_type=MESH)
    pl.semaphore_signal(barrier, inc=1, device_id={"pb": partner}, device_id_type=MESH)

    inputs = [
        pltpu.make_async_copy(src, dst, in_sem.at[n])
        for n, (src, dst) in enumerate(
            (
                (rows_hbm, chosen), (diff_hbm, diff), (label_hbm, label), (vir_hbm, vir_ref),
                (occ_hbm, occ_ref), (occ_e_hbm, occ_e), (vir_e_hbm, vir_e),
            )
        )
    ]
    for copy in inputs:
        copy.start()
    blocks = {s: pltpu.make_async_copy(ao_hbm.at[s], ao_ref.at[s], ao_sem.at[s]) for s in (0, 2, 1, 3)}
    for copy in blocks.values():
        copy.start()
    w_hi[...] = jnp.zeros_like(w_hi)
    w_lo[...] = jnp.zeros_like(w_lo)

    for copy in inputs:
        copy.wait()

    def energies():
        col = lax.broadcasted_iota(jnp.int32, (32, 64), 1)
        row = lax.broadcasted_iota(jnp.int32, (32, 64), 0)
        first_lanes = lax.broadcasted_iota(jnp.int32, (32, 128), 1) < 64

        def pick(values, k):
            lane = lax.broadcasted_iota(jnp.int32, values.shape, 1)
            return jnp.sum(jnp.where(lane == k, values, 0.0), axis=1, keepdims=True)

        for b in range(2):
            ki = chosen[b, pb]
            line = vir_e[pl.ds(diff[ki, label[pb]], 1), :]
            even = jnp.sum(jnp.where(col == 2 * row, line, 0.0), axis=1, keepdims=True)
            odd = jnp.sum(jnp.where(col == 2 * row + 1, line, 0.0), axis=1, keepdims=True)
            left = pick(occ_e[pl.ds(aux, 1), :], ki) - jnp.where(first_lanes, even, odd)
            for t in range(2):
                kj = chosen[2 + t, partner]
                right = vir_e[pl.ds(diff[kj, label[partner]], 1), :]
                base_ref[2 * b + t] = left - jnp.concatenate([right, right], 1)
                if b == 0:
                    occr_ref[t] = jnp.broadcast_to(pick(occ_e[...], kj), (16, 128))

    def make(s):
        blocks[s].wait()
        k = chosen[s, pb]
        ka = diff[k, label[pb]]
        occ = jnp.concatenate([occ_ref[k, 0], occ_ref[k, 1]], 0)

        def put(p, value):
            lr_ref.reshape(2560, 128)[pl.ds(s * 640 + p, 16, stride=40), :] = value

        orbitals(s, ao_ref, occ, vir_ref[ka, 0], vir_ref[ka, 1], put, w_hi, w_lo, x_hi, x_lo, t1)

    def place(pos, core):
        return pl.ds(pl.multiple_of(pos * 80 + core * 40, 8), 40)

    def chunk(pos, q):
        return rbuf.at[pl.ds(LINES * q, LINES), place(pos, c), :]

    def partner_copy(q):
        return pltpu.make_async_remote_copy(
            lr_ref.at[pl.ds(32 + LINES * q, LINES)], chunk(0, q), par_send.at[q], par_recv.at[q],
            device_id={"pb": partner}, device_id_type=MESH,
        )

    def hop_copy(way, d, q):
        step = 1 - 2 * way
        return pltpu.make_async_remote_copy(
            chunk(POS[-step * (d - 1)], q), chunk(POS[-step * d], q),
            hop_send.at[way, d - 1, q], hop_recv.at[way, d - 1, q],
            device_id={"aux": at_z(step, c)}, device_id_type=MESH,
        )

    def sibling_copy(pos, q):
        return pltpu.make_async_remote_copy(
            chunk(pos, q), chunk(pos, q), sib_send.at[pos, q], sib_recv.at[pos, q],
            device_id={"aux": sibling}, device_id_type=MESH,
        )

    def row_copy(s, dz, cross):
        core = c + cross * (1 - 2 * c)
        to = at_z(dz, core)
        pos = POS[-dz]
        src, dst = lr_ref.at[16 * s + to], lbuf.at[s, place(pos, c), :]
        if dz == 0 and cross == 0:
            return pltpu.make_async_copy(src, dst, own_sem.at[s])
        return pltpu.make_async_remote_copy(
            src, dst, l_send.at[s, pos, cross], l_recv.at[s, pos, cross],
            device_id={"aux": to}, device_id_type=MESH,
        )

    rows = {
        (s, dz, cross): row_copy(s, dz, cross)
        for s in range(2) for dz in (4, 3, -3, 2, -2, 1, -1, 0) for cross in range(2)
    }
    partners = [partner_copy(q) for q in range(CHUNKS)]
    sent = []

    def send(copy):
        copy.start()
        sent.append(copy)

    def send_rows(s):
        for (block, _, _), copy in rows.items():
            if block == s:
                copy.start()

    def send_partner(t):
        for q in range(CHUNKS):
            if q * LINES // 16 == t:
                partners[q].start()

    def has_hop(way, d, q):
        return d < 4 or q * LINES // 16 == way

    def relay(d, q):
        for way in range(2):
            if not has_hop(way, d, q):
                continue
            hop_copy(way, d, q).wait_recv()
            if d < 4 and has_hop(way, d + 1, q):
                send(hop_copy(way, d + 1, q))
            send(sibling_copy(POS[-d if way == 0 else d], q))

    def left_sides():
        for (s, dz, cross), copy in rows.items():
            if dz == 0 and cross == 0:
                copy.wait()
            else:
                copy.wait_recv()
        for n, (first, last) in enumerate(STAGES):
            for s in range(2):
                part = lbuf[s, first:last, :]
                part = jnp.concatenate([part, jnp.zeros((256 - (last - first), 128), F32)], 0)
                hi, lo = halves(part.T)
                lt_hi[n, 128 * s : 128 * s + 128, :] = hi
                lt_lo[n, 128 * s : 128 * s + 128, :] = lo

    low = lax.broadcasted_iota(jnp.int32, (32, 128), 1) < 64

    def finish(n):
        t, j = n // 16, n % 16
        for s in range(2):
            def half(part, odd):
                return ybuf[n, pl.ds(128 * s + 64 * part + odd, 32, stride=2), :]

            re_e, re_d, im_e, im_d = half(0, 0), half(0, 1), half(1, 0), half(1, 1)
            inverse = 1.0 / (base_ref[2 * s + t] + occr_ref[t, pl.ds(j, 1), :])
            real = jnp.where(low, re_e, swap_sides(re_d)) - jnp.where(low, swap_sides(im_e), im_d)
            imag = jnp.where(low, swap_sides(re_e), re_d) + jnp.where(low, im_e, swap_sides(im_d))
            for part, value in enumerate((real, imag)):
                first = ((part * 2 + s) * 2 + t) * 512 + (j // 8) * 256 + j % 8
                out_ref[pl.ds(first, 32, stride=8), :] = value * inverse

    def multiply(stage, q):
        first, last = STAGES[stage]
        width = last - first

        def body(pair, _):
            n = LINES * q + pair * 2
            r = jnp.concatenate([rbuf[n + h, first:last, :] for h in range(2)], 1)
            hi, lo = halves(r)
            lh, ll = lt_hi[stage, :, :width], lt_lo[stage, :, :width]
            y = dot(lh, hi) + dot(ll, hi) + dot(lh, lo)
            for h in range(2):
                value = y[:, 128 * h : 128 * h + 128]
                if stage > 0:
                    value = value + ybuf[n + h]
                ybuf[n + h] = value
                if stage == 2:
                    finish(n + h)
            return 0

        lax.fori_loop(0, LINES // 2, body, 0, unroll=4)

    def from_sibling(q, *positions):
        for pos in positions:
            sibling_copy(pos, q).wait_recv()

    def open_ring(q):
        partners[q].wait_recv()
        for way in range(2):
            send(hop_copy(way, 1, q))
        send(sibling_copy(0, q))

    make(0)
    pl.semaphore_wait(barrier, 16)
    send_rows(0)
    make(2)
    send_partner(0)
    energies()
    make(1)
    send_rows(1)
    make(3)
    send_partner(1)
    for q in range(CHUNKS):
        open_ring(q)
    for q in range(CHUNKS):
        relay(1, q)
    left_sides()
    for q in range(CHUNKS):
        relay(2, q)
        from_sibling(q, 0, 1, 2)
        multiply(0, q)
    for q in range(CHUNKS):
        relay(3, q)
        from_sibling(q, 3, 4)
        multiply(1, q)
    for half in range(CHUNKS // 2):
        for q in (half, half + CHUNKS // 2):
            relay(4, q)
        for q in (half, half + CHUNKS // 2):
            from_sibling(q, 5, 6, 7)
            multiply(2, q)
    for copy in partners + sent:
        copy.wait_send()
    for (s, dz, cross), copy in rows.items():
        if dz != 0 or cross != 0:
            copy.wait_send()


def pair_sums(*operands):
    dma = pltpu.SemaphoreType.DMA
    return pl.pallas_call(
        pair_kernel,
        out_shape=jax.ShapeDtypeStruct((4096, 128), F32),
        in_specs=[pl.BlockSpec(memory_space=pltpu.HBM)] * 8,
        out_specs=pl.BlockSpec(memory_space=pltpu.VMEM),
        scratch_shapes=[
            pltpu.VMEM((27, 2, 16, 80), F32),
            pltpu.VMEM((27, 2, 64, 80), F32),
            pltpu.VMEM((16, 27), F32),
            pltpu.VMEM((27, 64), F32),
            pltpu.SMEM((27, 27), jnp.int32),
            pltpu.SMEM((16,), jnp.int32),
            pltpu.SMEM((4, 16), jnp.int32),
            pltpu.VMEM((4, 32, 128), F32),
            pltpu.VMEM((2, 16, 128), F32),
            pltpu.VMEM((4, 4000, 128), F32),
            pltpu.VMEM((5, 256, 384), BF16),
            pltpu.VMEM((5, 256, 384), BF16),
            pltpu.VMEM((5, 400, 256), BF16),
            pltpu.VMEM((5, 400, 256), BF16),
            pltpu.VMEM((3200, 128), F32),
            pltpu.VMEM((64, 40, 128), F32),
            pltpu.VMEM((32, 640, 128), F32),
            pltpu.VMEM((2, 640, 128), F32),
            pltpu.VMEM((3, 256, 256), BF16),
            pltpu.VMEM((3, 256, 256), BF16),
            pltpu.VMEM((32, 256, 128), F32),
            dma((7,)),
            dma((4,)),
            dma((CHUNKS,)), dma((CHUNKS,)),
            dma((2, 4, CHUNKS)), dma((2, 4, CHUNKS)),
            dma((8, CHUNKS)), dma((8, CHUNKS)),
            dma((2, 8, 2)), dma((2, 8, 2)),
            dma((2,)),
        ],
        compiler_params=pltpu.CompilerParams(
            collective_id=0, has_side_effects=True, vmem_limit_bytes=56 * 2**20
        ),
        cost_estimate=pl.CostEstimate(flops=6 * 10**9, bytes_accessed=12 * 10**6, transcendentals=0),
        name="pair_sums",
    )(*operands)


def per_device(
    ao_blocks, occ_coef, vir_coef, occ_energy, vir_energy, kpoint_diff, transfer_label, chosen_rows
):
    ao = with_layout_constraint(
        ao_blocks.reshape(4, 40, 2, 50, 128), Layout(major_to_minor=(0, 1, 3, 2, 4))
    )
    ao = ao.transpose(0, 1, 3, 2, 4).reshape(4, 4000, 128)
    out = pair_sums(
        ao, occ_coef.swapaxes(2, 3), vir_coef.swapaxes(2, 3), occ_energy.T, vir_energy,
        kpoint_diff, transfer_label, chosen_rows.T,
    )
    out = out.reshape(2, 2, 2, 2, 32, 8, 128).transpose(0, 1, 2, 3, 5, 4, 6)
    return out.reshape(1, 2, 2, 2, 1, 16, 4096)


def solution(mesh):
    in_specs = (P("pb", None, "aux", None, None), P(), P(), P(), P(), P(), P(), P())
    out_specs = P("pb", None, None, None, "aux", None, None)
    return jax.shard_map(
        per_device, mesh=mesh, in_specs=in_specs, out_specs=out_specs, check_vma=False
    )
```
